32 devices in a mesh: groups: 2 (over x), space: 16 (over z, y, core).
Axes of the slice: x: 2, y: 2, z: 4, core: 2. Of those that a mesh axis runs over, the one named last changes fastest.
Arguments:
- features: bfloat16 [4, 16, 8, 512], P('groups', 'space'), parts along dimension 0, may hold values from -60 to 60, as said below
- norm_gain: float32 [512], replicated, may hold values from 0.5 to 1.5
- norm_bias: float32 [512], replicated, may hold values from -3 to 3
- query_weight: bfloat16 [512, 512], replicated, may hold values from -1 to 1
- query_bias: float32 [512], replicated, may hold values from -3 to 3
- key_weight: bfloat16 [512, 512], replicated, may hold values from -3 to 3
- value_weight: bfloat16 [512, 512], replicated, may hold values from -0.25 to 0.25
- value_bias: float32 [512], replicated, may hold values from -3 to 3
- out_weight: bfloat16 [512, 512], replicated, may hold values from -0.25 to 0.25
- out_bias: float32 [512], replicated, may hold values from -3 to 3
- conv_weight: bfloat16 [3, 3, 3, 512, 512], P(None, None, None, None, 'space'), may hold values from -0.0546875 to 0.0546875
- conv_bias: float32 [512], replicated, may hold values from -3 to 3
Outputs:
- decoded: bfloat16 [6, 32, 16, 512], P('groups', 'space'), parts along dimension 0
The draws below stay inside these ranges and needn't reach their ends.
There are 2 independent parts, one for each index of `groups`. The reference program is written for one: setup_inputs(seed, part) draws one part's arguments, and reference() takes and returns one part's arrays. A program takes and returns all parts, laid end to end along the dimension named above; an argument that names none is the same for every part. Nothing has to cross between parts.
Inputs may be any that keep to these rules, and one draw needn't show every extreme that they name: mid-block features of one video.
All inputs are finite; a program needn't handle non-finite values.
Results may differ from the reference program's by a relative error of at most 0.0079.
Values may be sent and summed in bfloat16 or wider, within the bound.
A program may use at most 128 MiB of HBM per device.

```python
import math
import jax
import jax.numpy as jnp
from jax import lax

C = 512
GROUPS = 32
FRAMES = 2
COLS = 8
HEIGHT = 16


def draw_features(key, part):
    noise_key, row_key = jax.random.split(key, 2)
    heights = jnp.arange(HEIGHT).astype(jnp.float32) / HEIGHT
    rising = (3.0 ** heights).reshape(1, HEIGHT, 1, 1)
    jitter = jnp.exp(jax.random.uniform(row_key, (1, HEIGHT, 1, 1), jnp.float32, -0.35, 0.35))
    full_shape = (FRAMES, HEIGHT, COLS, C)
    values = jax.random.truncated_normal(noise_key, -6.0, 6.0, full_shape, jnp.float32) * rising * jitter
    return values.astype(jnp.bfloat16)


def projection_pair(key):
    own_query = jax.random.truncated_normal(jax.random.fold_in(key, 12), -6.0, 6.0, (C, C), jnp.float32)
    own_key = jax.random.truncated_normal(jax.random.fold_in(key, 13), -6.0, 6.0, (C, C), jnp.float32)
    return (own_query, own_key)


def draw_query_weight(key, part):
    own_query, own_key = projection_pair(key)
    factor = C ** (-0.5)
    values = own_query * factor
    return values.astype(jnp.bfloat16)


def draw_key_weight(key, part):
    own_query, own_key = projection_pair(key)
    factor = C ** (-0.5)
    values = own_key * factor
    return values.astype(jnp.bfloat16)


def levels(rng, dims, shards, smallest, top_value):
    def one(axis_at, parts):
        steps = jax.random.uniform(jax.random.fold_in(jax.random.fold_in(rng, 6), axis_at), (parts,), jnp.float32, smallest / len(shards), top_value / len(shards))
        return jnp.repeat(jnp.exp(steps), dims[axis_at] // parts).reshape((-1,) + (1,) * (len(dims) - axis_at - 1))

    loudness = one(*shards[0])
    for cut in shards[1:]:
        loudness = loudness * one(*cut)
    return loudness


def normal_values(stream_key, shape, deviation, most, pieces=(), held_as=jnp.bfloat16):
    loudness = levels(stream_key, shape, pieces, -0.22, 0.18) if pieces else 1.0
    array = jax.random.normal(stream_key, shape, jnp.float32) * deviation * loudness
    return jnp.minimum(jnp.maximum(array, -most), most).astype(held_as)


def setup_inputs(seed: int = 0, part: int = 0) -> dict:
    key_list = jax.random.split(jax.random.key(seed), 13)
    own_keys = jax.random.split(jax.random.fold_in(key_list[12], part), 13)
    return {
        "features": draw_features(jax.random.fold_in(jax.random.fold_in(key_list[12], part), 71), part),
        "norm_gain": jnp.clip(1.0 + 0.1 * jax.random.normal(key_list[1], (C,), jnp.float32), 0.5, 1.5),
        "norm_bias": normal_values(key_list[2], (C,), 0.5, 3.0, (), jnp.float32),
        "query_weight": draw_query_weight(jax.random.fold_in(key_list[12], 71), part),
        "query_bias": normal_values(key_list[4], (C,), 0.5, 3.0, (), jnp.float32),
        "key_weight": draw_key_weight(jax.random.fold_in(key_list[12], 71), part),
        "value_weight": normal_values(key_list[6], (C, C), C ** -0.5, 0.25),
        "value_bias": normal_values(key_list[7], (C,), 0.5, 3.0, (), jnp.float32),
        "out_weight": normal_values(key_list[8], (C, C), C ** -0.5, 0.25),
        "out_bias": normal_values(key_list[9], (C,), 0.5, 3.0, (), jnp.float32),
        "conv_weight": normal_values(key_list[10], (3, 3, 3, C, C), (27 * C) ** -0.5, 0.0546875, ((4, 16),)),
        "conv_bias": normal_values(key_list[11], (C,), 0.5, 3.0, (), jnp.float32),
    }


EPSILON = 1e-06
NEGATIVE = -1e+30

def upsample_conv(row_band, weight):
    repeated = jnp.repeat(row_band[1:], 2, axis=0)
    frames = jnp.concatenate([row_band[:1], repeated], axis=0)
    doubled_rows = jnp.repeat(frames, 2, axis=1)[:, 1:-1]
    columns = jnp.repeat(doubled_rows, 2, axis=2)
    columns = jnp.concatenate([columns[:, :, :1], columns, columns[:, :, -1:]], axis=2)
    padded = jnp.concatenate([columns[:1], columns[:1], columns], axis=0)
    out_frames = frames.shape[0]
    out_rows = doubled_rows.shape[1] - 2
    out_cols = columns.shape[2] - 2
    channels = row_band.shape[3]
    out_width = weight.shape[4]
    result = jnp.zeros((out_frames * out_rows * out_cols, out_width), jnp.float32)
    for time_tap in range(3):
        for row_tap in range(3):
            for col_tap in range(3):
                window = padded[time_tap:time_tap + out_frames, row_tap:row_tap + out_rows, col_tap:col_tap + out_cols]
                result = result + jnp.dot(window.reshape(-1, channels), weight[time_tap, row_tap, col_tap], preferred_element_type=jnp.float32)
    return result.reshape(out_frames, out_rows, out_cols, out_width)

def reference(features, norm_gain, norm_bias, query_weight, query_bias, key_weight, value_weight, value_bias, out_weight, out_bias, conv_weight, conv_bias):
    grouped = features.astype(jnp.float32).reshape(-1, GROUPS, C // GROUPS)
    group_mean = lax.optimization_barrier(jnp.mean(grouped, axis=(0, 2)))
    centred = grouped - group_mean[None, :, None]
    variance = lax.optimization_barrier(jnp.mean(centred * centred, axis=(0, 2)))
    normed = ((centred * lax.rsqrt(variance + EPSILON)[None, :, None]).reshape(-1, C) * norm_gain + norm_bias).astype(jnp.bfloat16)
    softmax_scale = C ** (-0.5)
    queries = ((jnp.dot(normed, query_weight, preferred_element_type=jnp.float32) + query_bias) * softmax_scale).astype(jnp.bfloat16)
    key_rows = jnp.dot(normed, key_weight, preferred_element_type=jnp.float32).astype(jnp.bfloat16)
    value_rows = (jnp.dot(normed, value_weight, preferred_element_type=jnp.float32) + value_bias).astype(jnp.bfloat16)
    token_count = FRAMES * HEIGHT * COLS
    query_block = math.gcd(512, token_count)
    frame_of = (jnp.arange(token_count) // (HEIGHT * COLS)).astype(jnp.int32)

    def attend(number):
        block_queries = lax.dynamic_slice_in_dim(queries, number * query_block, query_block, 0)
        block_frames = lax.dynamic_slice_in_dim(frame_of, number * query_block, query_block, 0)
        scores = jnp.dot(block_queries, key_rows.T, preferred_element_type=jnp.float32)
        allowed = block_frames[:, None] >= frame_of[None, :]
        scores = jnp.where(allowed, scores, NEGATIVE)
        running_max = lax.optimization_barrier(jnp.max(scores, axis=1, keepdims=True))
        weights = jnp.where(allowed, jnp.exp(scores - running_max), 0.0)
        denominator = lax.optimization_barrier(jnp.sum(weights, axis=1, keepdims=True))
        summed = jnp.dot(weights.astype(jnp.bfloat16), value_rows, preferred_element_type=jnp.float32)
        return (summed / denominator).astype(jnp.bfloat16)
    attended = lax.map(attend, jnp.arange(token_count // query_block).astype(jnp.int32)).reshape(-1, C)
    mixed_tokens = (features.reshape(-1, C).astype(jnp.float32) + jnp.dot(attended, out_weight, preferred_element_type=jnp.float32) + out_bias).astype(jnp.bfloat16)
    mixed_tokens = mixed_tokens.reshape(FRAMES, HEIGHT, COLS, C)
    row_band = jnp.concatenate([mixed_tokens[:, :1], mixed_tokens, mixed_tokens[:, -1:]], axis=1)
    convolved = upsample_conv(row_band, conv_weight)
    return (convolved + conv_bias).astype(jnp.bfloat16)
```

```python
import functools

import jax
import jax.numpy as jnp
from jax import lax
from jax.experimental import pallas as pl
from jax.experimental.pallas import tpu as pltpu
from jax.sharding import PartitionSpec as P

GROUPS = 32


EPSILON = 1e-06
NEGATIVE = -1e30


def with_halo(value, sides, width):
    for axis, dim in sides:
        count, length = (lax.axis_size(axis), value.shape[dim])
        up = [(i, (i + 1) % count) for i in range(count - 1)]
        down = [(j, i) for i, j in up]
        last = lax.slice_in_dim(value, length - width, length, axis=dim)
        leading = lax.slice_in_dim(value, 0, width, axis=dim)
        before = lax.ppermute(last, axis, up)
        after = lax.ppermute(leading, axis, down)
        value = jnp.concatenate([before, value, after], axis=dim)
    return value


def upsample_conv(row_band, weight):
    repeated = jnp.repeat(row_band[1:], 2, axis=0)
    frames = jnp.concatenate([row_band[:1], repeated], axis=0)
    doubled_rows = jnp.repeat(frames, 2, axis=1)[:, 1:-1]
    columns = jnp.repeat(doubled_rows, 2, axis=2)
    columns = jnp.concatenate([columns[:, :, :1], columns, columns[:, :, -1:]], axis=2)
    padded = jnp.concatenate([columns[:1], columns[:1], columns], axis=0)
    out_frames = frames.shape[0]
    out_rows = doubled_rows.shape[1] - 2
    out_cols = columns.shape[2] - 2
    channels = row_band.shape[3]
    out_width = weight.shape[4]
    result = jnp.zeros((out_frames * out_rows * out_cols, out_width), jnp.float32)
    for time_tap in range(3):
        for row_tap in range(3):
            for col_tap in range(3):
                window = padded[
                    time_tap : time_tap + out_frames,
                    row_tap : row_tap + out_rows,
                    col_tap : col_tap + out_cols,
                ]
                result = result + jnp.dot(
                    window.reshape(-1, channels),
                    weight[time_tap, row_tap, col_tap],
                    preferred_element_type=jnp.float32,
                )
    return result.reshape(out_frames, out_rows, out_cols, out_width)


def per_device_sharded(
    features,
    norm_gain,
    norm_bias,
    query_weight,
    query_bias,
    key_weight,
    value_weight,
    value_bias,
    out_weight,
    out_bias,
    conv_weight,
    conv_bias,
):
    frames, local_rows, columns, channels = features.shape
    spread = lax.axis_size("space")
    grouped = features.astype(jnp.float32).reshape(-1, GROUPS, channels // GROUPS)
    entries = grouped.shape[0] * grouped.shape[2] * spread
    group_mean = lax.psum(jnp.sum(grouped, axis=(0, 2)), "space") / entries
    centred = grouped - group_mean[None, :, None]
    variance = lax.psum(jnp.sum(centred * centred, axis=(0, 2)), "space") / entries
    normed = (
        (centred * lax.rsqrt(variance + EPSILON)[None, :, None]).reshape(-1, channels) * norm_gain
        + norm_bias
    ).astype(jnp.bfloat16)
    softmax_scale = channels ** (-0.5)
    queries = (
        (jnp.dot(normed, query_weight, preferred_element_type=jnp.float32) + query_bias)
        * softmax_scale
    ).astype(jnp.bfloat16)
    key_tiles = (
        jnp.dot(normed, key_weight, preferred_element_type=jnp.float32)
        .astype(jnp.bfloat16)
        .reshape(frames, local_rows, columns, channels)
    )
    value_tiles = (
        (jnp.dot(normed, value_weight, preferred_element_type=jnp.float32) + value_bias)
        .astype(jnp.bfloat16)
        .reshape(frames, local_rows, columns, channels)
    )
    local_count = queries.shape[0]
    query_frame = jnp.arange(local_count) // (local_rows * columns)
    running_max = jnp.full((local_count,), NEGATIVE, jnp.float32)
    key_piece = lax.all_gather(key_tiles, "space", axis=1, tiled=True)
    value_piece = lax.all_gather(value_tiles, "space", axis=1, tiled=True)
    per_frame = key_piece.shape[1] * key_piece.shape[2]
    key_rows = key_piece.reshape(-1, channels)
    value_rows = value_piece.reshape(-1, channels)
    key_frame = jnp.arange(key_rows.shape[0]) // per_frame
    allowed = query_frame[:, None] >= key_frame[None, :]
    scores = jnp.where(
        allowed, jnp.dot(queries, key_rows.T, preferred_element_type=jnp.float32), NEGATIVE
    )
    new_max = jnp.maximum(running_max, jnp.max(scores, axis=1))
    weights = jnp.where(allowed, jnp.exp(scores - new_max[:, None]), 0.0)
    denominator = jnp.sum(weights, axis=1)
    weighted = jnp.dot(weights.astype(jnp.bfloat16), value_rows, preferred_element_type=jnp.float32)
    running_max, denominator, weighted = (new_max, denominator, weighted)
    attended = (weighted / denominator[:, None]).astype(jnp.bfloat16)
    mixed_tokens = (
        features.reshape(-1, channels).astype(jnp.float32)
        + jnp.dot(attended, out_weight, preferred_element_type=jnp.float32)
        + out_bias
    ).astype(jnp.bfloat16)
    mixed_tokens = mixed_tokens.reshape(frames, local_rows, columns, channels)
    rimmed = with_halo(mixed_tokens, (("space", 1),), 1)
    position = lax.axis_index("space")
    upper_rim = jnp.where(position == 0, mixed_tokens, rimmed[:, :1])
    lower_rim = jnp.where(position == spread - 1, mixed_tokens, rimmed[:, -1:])
    row_band = jnp.concatenate([upper_rim, mixed_tokens, lower_rim], axis=1)
    convolved = upsample_conv(row_band, lax.all_gather(conv_weight, "space", axis=4, tiled=True))
    decoded = (convolved + conv_bias).astype(jnp.bfloat16)
    return decoded


MESH = pl.DeviceIdType.MESH
F32 = jnp.float32
BF16 = jnp.bfloat16


def dot_t(a, b):
    return lax.dot_general(a, b, (((1,), (1,)), ((), ())), preferred_element_type=F32)


def dot_n(a, b):
    return jnp.dot(a, b, preferred_element_type=F32)


def group_total(row, width):
    channels = row.shape[1]
    lane = lax.broadcasted_iota(jnp.int32, row.shape, 1)
    step = 1
    while step < width:
        high = (lane // step) % 2 == 1
        row = row + jnp.where(
            high, pltpu.roll(row, step, 1), pltpu.roll(row, channels - step, 1)
        )
        step *= 2
    return row


def fold_conv_weights(conv_v, w0_ref, w1_ref):
    outs, channels = conv_v.shape[1], conv_v.shape[2]
    zero = jnp.zeros((outs, channels), BF16)
    combos = (
        (w0_ref, 0, (0, 1, 2)),
        (w0_ref, 1, (0, 1)),
        (w0_ref, 2, (0,)),
        (w1_ref, 0, (2,)),
        (w1_ref, 1, (1, 2)),
    )
    spatial = {
        (0, 0): (0,),
        (0, 1): (1, 2),
        (1, 1): (0, 1),
        (1, 2): (2,),
    }
    for ref, slot, times in combos:
        summed = {}
        for b in range(3):
            for e in range(3):
                value = conv_v[times[0] * 9 + b * 3 + e].astype(F32)
                for a in times[1:]:
                    value = value + conv_v[a * 9 + b * 3 + e].astype(F32)
                summed[b, e] = value
        for p in range(2):
            for dr in range(3):
                rows = spatial.get((p, dr))
                if rows is not None:
                    by_col = []
                    for e in range(3):
                        value = summed[rows[0], e]
                        for b in rows[1:]:
                            value = value + summed[b, e]
                        by_col.append(value)
                for q in range(2):
                    for dc in range(3):
                        cols = spatial.get((q, dc))
                        if rows is None or cols is None:
                            piece = zero
                        else:
                            value = by_col[cols[0]]
                            for e in cols[1:]:
                                value = value + by_col[e]
                            piece = value.astype(BF16)
                        at = slot * 4 * outs + (p * 2 + q) * outs
                        tap = (dr * 3 + dc) * channels
                        ref[at : at + outs, tap : tap + channels] = piece


def shifted_inputs(frame, x_ref):
    height, width, channels = frame.shape
    column = lax.broadcasted_iota(jnp.int32, frame.shape, 1)
    left = jnp.where(column == 0, frame, jnp.roll(frame, 1, axis=1))
    right = jnp.where(column == width - 1, frame, jnp.roll(frame, -1, axis=1))
    for dc, plane in enumerate((left, frame, right)):
        up = jnp.concatenate([plane[:1], plane[:-1]], axis=0)
        down = jnp.concatenate([plane[1:], plane[-1:]], axis=0)
        for dr, moved in enumerate((up, plane, down)):
            tap = (dr * 3 + dc) * channels
            x_ref[:, tap : tap + channels] = moved.reshape(height * width, channels).astype(BF16)


def fused_kernel(
    count,
    feat_ref,
    gain_ref,
    nbias_ref,
    qw_ref,
    qb_ref,
    kw_ref,
    vw_ref,
    vb_ref,
    ow_ref,
    ob_ref,
    cw_ref,
    cb_ref,
    out_ref,
    gath,
    qw,
    kw,
    vw,
    ow,
    cw,
    w0_ref,
    w1_ref,
    x0_ref,
    x1_ref,
    sendbuf,
    recvbuf,
    wide,
    load_sem,
    fsend_sem,
    frecv_sem,
    osend_sem,
    orecv_sem,
):
    me = lax.axis_index("space")
    chips = count // 2
    sibling = me + 1 - 2 * lax.rem(me, 2)
    width, channels = feat_ref.shape[0] // 2, feat_ref.shape[1]

    barrier = pltpu.get_barrier_semaphore()
    for k in range(1, count):
        pl.semaphore_signal(
            barrier, inc=1, device_id={"space": lax.rem(me + k, count)}, device_id_type=MESH
        )
    loads = [
        pltpu.make_async_copy(s, d, load_sem.at[i])
        for i, (s, d) in enumerate(
            ((feat_ref, gath.at[me]), (cw_ref, cw), (qw_ref, qw), (kw_ref, kw), (vw_ref, vw), (ow_ref, ow))
        )
    ]
    for load in loads:
        load.start()
    pl.semaphore_wait(barrier, count - 1)

    def feat_copy(src, block, to, slot):
        return pltpu.make_async_remote_copy(
            src_ref=src,
            dst_ref=gath.at[block],
            send_sem=fsend_sem.at[slot],
            recv_sem=frecv_sem.at[block],
            device_id={"space": to},
            device_id_type=MESH,
        )

    sends = [
        feat_copy(feat_ref, me, lax.rem(me + 2 * k, count), k) for k in range(1, chips)
    ] + [feat_copy(feat_ref, me, sibling, 0)]
    for send in sends:
        send.start()

    loads[1].wait()
    fold_conv_weights(cw, w0_ref, w1_ref)

    for k in range(1, chips):
        block = lax.rem(me + count - 2 * k, count)
        feat_copy(feat_ref, block, sibling, 0).wait_recv()
        forward = feat_copy(gath.at[block], block, sibling, chips + k)
        forward.start()
        sends.append(forward)
    loads[0].wait()
    for k in range(chips):
        block = lax.rem(sibling + count - 2 * k, count)
        feat_copy(feat_ref, block, sibling, 0).wait_recv()

    tokens = count * 2 * width
    feats = gath[...].reshape(tokens, channels).astype(F32)
    group_width = channels // GROUPS
    entries = tokens * group_width
    column = jnp.broadcast_to(jnp.sum(feats, axis=0, keepdims=True), (8, channels))
    mean = group_total(column, group_width)[:1] / entries
    centred = feats - mean
    column = jnp.broadcast_to(jnp.sum(centred * centred, axis=0, keepdims=True), (8, channels))
    variance = group_total(column, group_width)[:1] / entries
    normed = (centred * lax.rsqrt(variance + EPSILON) * gain_ref[...] + nbias_ref[...]).astype(BF16)
    for load in loads[2:]:
        load.wait()
    queries = ((dot_n(normed, qw[...]) + qb_ref[...]) * channels ** (-0.5)).astype(BF16)
    keys = dot_n(normed, kw[...]).astype(BF16)
    values = (dot_n(normed, vw[...]) + vb_ref[...]).astype(BF16)
    scores = dot_t(queries, keys)
    query_frame = (lax.broadcasted_iota(jnp.int32, scores.shape, 0) // width) % 2
    key_frame = (lax.broadcasted_iota(jnp.int32, scores.shape, 1) // width) % 2
    allowed = query_frame >= key_frame
    scores = jnp.where(allowed, scores, NEGATIVE)
    top = jnp.max(scores, axis=1, keepdims=True)
    weights = jnp.where(allowed, jnp.exp(scores - top), 0.0)
    denominator = jnp.sum(weights, axis=1, keepdims=True)
    attended = (dot_n(weights.astype(BF16), values) / denominator).astype(BF16)
    mixed = (
        gath[...].reshape(tokens, channels).astype(F32) + dot_n(attended, ow[...]) + ob_ref[...]
    )
    mixed = mixed.astype(BF16).astype(F32).reshape(count, 2, width, channels)
    shifted_inputs(mixed[:, 0], x0_ref)
    shifted_inputs(mixed[:, 1], x1_ref)

    outs = cw_ref.shape[1]
    lanes = 4 * outs
    bias_row = jnp.broadcast_to(cb_ref[...], (8, channels))
    own = jnp.zeros((8, outs), F32)
    for k in range(count):
        own = jnp.where(me == k, bias_row[:, k * outs : (k + 1) * outs], own)
    bias = jnp.concatenate([own] * 4, axis=1)[:1]
    first = dot_t(x0_ref[...], w0_ref[...])
    second = dot_t(x1_ref[...], w1_ref[...])
    frames = [
        first[:, :lanes] + bias,
        first[:, lanes : 2 * lanes] + second[:, :lanes] + bias,
        first[:, 2 * lanes :] + second[:, lanes:] + bias,
    ]
    frames = [f.reshape(count, width, lanes) for f in frames]
    packed = jnp.concatenate(frames + [jnp.zeros_like(frames[0])], axis=1)
    sendbuf[...] = packed.astype(BF16)

    def out_copy(row, source, to, slot):
        return pltpu.make_async_remote_copy(
            src_ref=sendbuf.at[row],
            dst_ref=recvbuf.at[source],
            send_sem=osend_sem.at[slot],
            recv_sem=orecv_sem.at[source],
            device_id={"space": to},
            device_id_type=MESH,
        )

    for k in range(1, count):
        to = lax.rem(me + k, count)
        send = out_copy(to, me, to, k)
        send.start()
        sends.append(send)
    own_copy = pltpu.make_async_copy(sendbuf.at[me], recvbuf.at[me], osend_sem.at[0])
    own_copy.start()
    own_copy.wait()
    for k in range(1, count):
        source = lax.rem(me + count - k, count)
        out_copy(source, source, me, k).wait_recv()

    each = 128 // outs
    for j in range(count // each):
        parts = [recvbuf[j * each + i].astype(F32) for i in range(each)]
        for p in range(2):
            for q in range(2):
                at = (p * 2 + q) * outs
                joined = jnp.concatenate([part[:, at : at + outs] for part in parts], axis=1)
                for t in range(3):
                    base = (t * 2 + p) * 2 * width + q
                    wide[j, pl.ds(base, width, stride=2), :] = joined[t * width : (t + 1) * width]
    for j in range(count // each):
        out_ref[:, j * 128 : (j + 1) * 128] = wide[j].astype(BF16)
    for send in sends:
        send.wait_send()


def per_device_fused(
    features,
    norm_gain,
    norm_bias,
    query_weight,
    query_bias,
    key_weight,
    value_weight,
    value_bias,
    out_weight,
    out_bias,
    conv_weight,
    conv_bias,
):
    count = lax.axis_size("space")
    frames, _, width, channels = features.shape
    outs = conv_weight.shape[4]
    rows = count * width
    taps = jnp.swapaxes(conv_weight, 3, 4).reshape(27, outs, channels)
    vmem = pl.BlockSpec(memory_space=pltpu.VMEM)
    hbm = pl.BlockSpec(memory_space=pl.ANY)
    square = pltpu.VMEM((channels, channels), BF16)
    row = lambda v: v.reshape(1, channels)
    out_rows = 3 * 2 * 2 * width
    decoded = pl.pallas_call(
        functools.partial(fused_kernel, count),
        out_shape=jax.ShapeDtypeStruct((out_rows, channels), BF16),
        in_specs=[hbm, vmem, vmem, hbm, vmem, hbm, hbm, vmem, hbm, vmem, hbm, vmem],
        out_specs=vmem,
        scratch_shapes=[
            pltpu.VMEM((count, frames * width, channels), BF16),
            square,
            square,
            square,
            square,
            pltpu.VMEM((27, outs, channels), BF16),
            pltpu.VMEM((12 * outs, 9 * channels), BF16),
            pltpu.VMEM((8 * outs, 9 * channels), BF16),
            pltpu.VMEM((rows, 9 * channels), BF16),
            pltpu.VMEM((rows, 9 * channels), BF16),
            pltpu.VMEM((count, 4 * width, 4 * outs), BF16),
            pltpu.VMEM((count, 4 * width, 4 * outs), BF16),
            pltpu.VMEM((channels // 128, out_rows, 128), F32),
            pltpu.SemaphoreType.DMA((6,)),
            pltpu.SemaphoreType.DMA((count,)),
            pltpu.SemaphoreType.DMA((count,)),
            pltpu.SemaphoreType.DMA((count,)),
            pltpu.SemaphoreType.DMA((count,)),
        ],
        compiler_params=pltpu.CompilerParams(
            collective_id=0, has_side_effects=True, vmem_limit_bytes=44 * 1024 * 1024
        ),
    )(
        features.reshape(frames * width, channels),
        row(norm_gain),
        row(norm_bias),
        query_weight,
        row(query_bias),
        key_weight,
        value_weight,
        row(value_bias),
        out_weight,
        row(out_bias),
        taps,
        row(conv_bias),
    )
    return decoded.reshape(3, 2, 2 * width, channels)


def per_device(features, *rest):
    count = lax.axis_size("space")
    frames, local_rows, width, channels = features.shape
    outs = rest[9].shape[4]
    if (frames, local_rows, width) == (2, 1, 8) and outs == 32 and count % 4 == 0:
        return per_device_fused(features, *rest)
    return per_device_sharded(features, *rest)


def solution(mesh):
    placed = (
        P("groups", "space", None, None),
        P(),
        P(),
        P(),
        P(),
        P(),
        P(),
        P(),
        P(),
        P(),
        P(None, None, None, None, "space"),
        P(),
    )
    return jax.shard_map(
        per_device,
        mesh=mesh,
        in_specs=placed,
        out_specs=P("groups", "space", None, None),
        check_vma=False,
    )
```

```python
import functools

import jax
import jax.numpy as jnp
from jax import lax
from jax.experimental import pallas as pl
from jax.experimental.pallas import tpu as pltpu
from jax.sharding import PartitionSpec as P

GROUPS = 32


EPSILON = 1e-06
NEGATIVE = -1e30


def with_halo(value, sides, width):
    for axis, dim in sides:
        count, length = (lax.axis_size(axis), value.shape[dim])
        up = [(i, (i + 1) % count) for i in range(count - 1)]
        down = [(j, i) for i, j in up]
        last = lax.slice_in_dim(value, length - width, length, axis=dim)
        leading = lax.slice_in_dim(value, 0, width, axis=dim)
        before = lax.ppermute(last, axis, up)
        after = lax.ppermute(leading, axis, down)
        value = jnp.concatenate([before, value, after], axis=dim)
    return value


def upsample_conv(row_band, weight):
    repeated = jnp.repeat(row_band[1:], 2, axis=0)
    frames = jnp.concatenate([row_band[:1], repeated], axis=0)
    doubled_rows = jnp.repeat(frames, 2, axis=1)[:, 1:-1]
    columns = jnp.repeat(doubled_rows, 2, axis=2)
    columns = jnp.concatenate([columns[:, :, :1], columns, columns[:, :, -1:]], axis=2)
    padded = jnp.concatenate([columns[:1], columns[:1], columns], axis=0)
    out_frames = frames.shape[0]
    out_rows = doubled_rows.shape[1] - 2
    out_cols = columns.shape[2] - 2
    channels = row_band.shape[3]
    out_width = weight.shape[4]
    result = jnp.zeros((out_frames * out_rows * out_cols, out_width), jnp.float32)
    for time_tap in range(3):
        for row_tap in range(3):
            for col_tap in range(3):
                window = padded[
                    time_tap : time_tap + out_frames,
                    row_tap : row_tap + out_rows,
                    col_tap : col_tap + out_cols,
                ]
                result = result + jnp.dot(
                    window.reshape(-1, channels),
                    weight[time_tap, row_tap, col_tap],
                    preferred_element_type=jnp.float32,
                )
    return result.reshape(out_frames, out_rows, out_cols, out_width)


def per_device_sharded(
    features,
    norm_gain,
    norm_bias,
    query_weight,
    query_bias,
    key_weight,
    value_weight,
    value_bias,
    out_weight,
    out_bias,
    conv_weight,
    conv_bias,
):
    frames, local_rows, columns, channels = features.shape
    spread = lax.axis_size("space")
    grouped = features.astype(jnp.float32).reshape(-1, GROUPS, channels // GROUPS)
    entries = grouped.shape[0] * grouped.shape[2] * spread
    group_mean = lax.psum(jnp.sum(grouped, axis=(0, 2)), "space") / entries
    centred = grouped - group_mean[None, :, None]
    variance = lax.psum(jnp.sum(centred * centred, axis=(0, 2)), "space") / entries
    normed = (
        (centred * lax.rsqrt(variance + EPSILON)[None, :, None]).reshape(-1, channels) * norm_gain
        + norm_bias
    ).astype(jnp.bfloat16)
    softmax_scale = channels ** (-0.5)
    queries = (
        (jnp.dot(normed, query_weight, preferred_element_type=jnp.float32) + query_bias)
        * softmax_scale
    ).astype(jnp.bfloat16)
    key_tiles = (
        jnp.dot(normed, key_weight, preferred_element_type=jnp.float32)
        .astype(jnp.bfloat16)
        .reshape(frames, local_rows, columns, channels)
    )
    value_tiles = (
        (jnp.dot(normed, value_weight, preferred_element_type=jnp.float32) + value_bias)
        .astype(jnp.bfloat16)
        .reshape(frames, local_rows, columns, channels)
    )
    local_count = queries.shape[0]
    query_frame = jnp.arange(local_count) // (local_rows * columns)
    running_max = jnp.full((local_count,), NEGATIVE, jnp.float32)
    key_piece = lax.all_gather(key_tiles, "space", axis=1, tiled=True)
    value_piece = lax.all_gather(value_tiles, "space", axis=1, tiled=True)
    per_frame = key_piece.shape[1] * key_piece.shape[2]
    key_rows = key_piece.reshape(-1, channels)
    value_rows = value_piece.reshape(-1, channels)
    key_frame = jnp.arange(key_rows.shape[0]) // per_frame
    allowed = query_frame[:, None] >= key_frame[None, :]
    scores = jnp.where(
        allowed, jnp.dot(queries, key_rows.T, preferred_element_type=jnp.float32), NEGATIVE
    )
    new_max = jnp.maximum(running_max, jnp.max(scores, axis=1))
    weights = jnp.where(allowed, jnp.exp(scores - new_max[:, None]), 0.0)
    denominator = jnp.sum(weights, axis=1)
    weighted = jnp.dot(weights.astype(jnp.bfloat16), value_rows, preferred_element_type=jnp.float32)
    running_max, denominator, weighted = (new_max, denominator, weighted)
    attended = (weighted / denominator[:, None]).astype(jnp.bfloat16)
    mixed_tokens = (
        features.reshape(-1, channels).astype(jnp.float32)
        + jnp.dot(attended, out_weight, preferred_element_type=jnp.float32)
        + out_bias
    ).astype(jnp.bfloat16)
    mixed_tokens = mixed_tokens.reshape(frames, local_rows, columns, channels)
    rimmed = with_halo(mixed_tokens, (("space", 1),), 1)
    position = lax.axis_index("space")
    upper_rim = jnp.where(position == 0, mixed_tokens, rimmed[:, :1])
    lower_rim = jnp.where(position == spread - 1, mixed_tokens, rimmed[:, -1:])
    row_band = jnp.concatenate([upper_rim, mixed_tokens, lower_rim], axis=1)
    convolved = upsample_conv(row_band, lax.all_gather(conv_weight, "space", axis=4, tiled=True))
    decoded = (convolved + conv_bias).astype(jnp.bfloat16)
    return decoded


MESH = pl.DeviceIdType.MESH
F32 = jnp.float32
BF16 = jnp.bfloat16


def dot_t(a, b):
    return lax.dot_general(a, b, (((1,), (1,)), ((), ())), preferred_element_type=F32)


def dot_n(a, b):
    return jnp.dot(a, b, preferred_element_type=F32)


def group_total(row, width):
    channels = row.shape[1]
    lane = lax.broadcasted_iota(jnp.int32, row.shape, 1)
    step = 1
    while step < width:
        high = (lane // step) % 2 == 1
        row = row + jnp.where(
            high, pltpu.roll(row, step, 1), pltpu.roll(row, channels - step, 1)
        )
        step *= 2
    return row


def fold_conv_weights(conv_v, w0_ref, w1_ref):
    outs, channels = conv_v.shape[1], conv_v.shape[2]
    zero = jnp.zeros((outs, channels), BF16)
    combos = (
        (w0_ref, 0, (0, 1, 2)),
        (w0_ref, 1, (0, 1)),
        (w0_ref, 2, (0,)),
        (w1_ref, 0, (2,)),
        (w1_ref, 1, (1, 2)),
    )
    spatial = {
        (0, 0): (0,),
        (0, 1): (1, 2),
        (1, 1): (0, 1),
        (1, 2): (2,),
    }
    for ref, slot, times in combos:
        summed = {}
        for b in range(3):
            for e in range(3):
                value = conv_v[times[0] * 9 + b * 3 + e].astype(F32)
                for a in times[1:]:
                    value = value + conv_v[a * 9 + b * 3 + e].astype(F32)
                summed[b, e] = value
        for p in range(2):
            for dr in range(3):
                rows = spatial.get((p, dr))
                if rows is not None:
                    by_col = []
                    for e in range(3):
                        value = summed[rows[0], e]
                        for b in rows[1:]:
                            value = value + summed[b, e]
                        by_col.append(value)
                for q in range(2):
                    for dc in range(3):
                        cols = spatial.get((q, dc))
                        if rows is None or cols is None:
                            piece = zero
                        else:
                            value = by_col[cols[0]]
                            for e in cols[1:]:
                                value = value + by_col[e]
                            piece = value.astype(BF16)
                        at = slot * 4 * outs + (p * 2 + q) * outs
                        tap = (dr * 3 + dc) * channels
                        ref[at : at + outs, tap : tap + channels] = piece


def shifted_inputs(frame, x_ref):
    height, width, channels = frame.shape
    column = lax.broadcasted_iota(jnp.int32, frame.shape, 1)
    left = jnp.where(column == 0, frame, jnp.roll(frame, 1, axis=1))
    right = jnp.where(column == width - 1, frame, jnp.roll(frame, -1, axis=1))
    for dc, plane in enumerate((left, frame, right)):
        up = jnp.concatenate([plane[:1], plane[:-1]], axis=0)
        down = jnp.concatenate([plane[1:], plane[-1:]], axis=0)
        for dr, moved in enumerate((up, plane, down)):
            tap = (dr * 3 + dc) * channels
            x_ref[:, tap : tap + channels] = moved.reshape(height * width, channels).astype(BF16)


def fused_kernel(
    count,
    feat_ref,
    gain_ref,
    nbias_ref,
    qw_ref,
    qb_ref,
    kw_ref,
    vw_ref,
    vb_ref,
    ow_ref,
    ob_ref,
    cw_ref,
    cb_ref,
    out_ref,
    gath,
    qw,
    kw,
    vw,
    ow,
    cw,
    gain,
    nbias,
    qb,
    vb,
    ob,
    cb,
    w0_ref,
    w1_ref,
    x0_ref,
    x1_ref,
    sendbuf,
    recvbuf,
    wide,
    load_sem,
    fsend_sem,
    frecv_sem,
    osend_sem,
    orecv_sem,
):
    me = lax.axis_index("space")
    chips = count // 2
    sibling = me + 1 - 2 * lax.rem(me, 2)
    width, channels = feat_ref.shape[0] // 2, feat_ref.shape[1]

    barrier = pltpu.get_barrier_semaphore()
    for k in range(1, count):
        pl.semaphore_signal(
            barrier, inc=1, device_id={"space": lax.rem(me + k, count)}, device_id_type=MESH
        )
    loads = [
        pltpu.make_async_copy(s, d, load_sem.at[i])
        for i, (s, d) in enumerate(
            (
                (feat_ref, gath.at[me]),
                (cw_ref, cw),
                (gain_ref, gain),
                (nbias_ref, nbias),
                (qw_ref, qw),
                (kw_ref, kw),
                (vw_ref, vw),
                (ow_ref, ow),
                (qb_ref, qb),
                (vb_ref, vb),
                (ob_ref, ob),
                (cb_ref, cb),
            )
        )
    ]
    for load in loads:
        load.start()
    pl.semaphore_wait(barrier, count - 1)

    def feat_copy(src, block, to, slot):
        return pltpu.make_async_remote_copy(
            src_ref=src,
            dst_ref=gath.at[block],
            send_sem=fsend_sem.at[slot],
            recv_sem=frecv_sem.at[block],
            device_id={"space": to},
            device_id_type=MESH,
        )

    sends = [
        feat_copy(feat_ref, me, lax.rem(me + 2 * k, count), k) for k in range(1, chips)
    ] + [feat_copy(feat_ref, me, sibling, 0)]
    for send in sends:
        send.start()

    loads[1].wait()
    fold_conv_weights(cw, w0_ref, w1_ref)

    for k in range(1, chips):
        block = lax.rem(me + count - 2 * k, count)
        feat_copy(feat_ref, block, sibling, 0).wait_recv()
        forward = feat_copy(gath.at[block], block, sibling, chips + k)
        forward.start()
        sends.append(forward)
    for load in loads[2:]:
        load.wait()
    loads[0].wait()
    for k in range(chips):
        block = lax.rem(sibling + count - 2 * k, count)
        feat_copy(feat_ref, block, sibling, 0).wait_recv()

    tokens = count * 2 * width
    feats = gath[...].reshape(tokens, channels).astype(F32)
    group_width = channels // GROUPS
    entries = tokens * group_width
    column = jnp.broadcast_to(jnp.sum(feats, axis=0, keepdims=True), (8, channels))
    mean = group_total(column, group_width)[:1] / entries
    centred = feats - mean
    column = jnp.broadcast_to(jnp.sum(centred * centred, axis=0, keepdims=True), (8, channels))
    variance = group_total(column, group_width)[:1] / entries
    normed = (centred * lax.rsqrt(variance + EPSILON) * gain[...] + nbias[...]).astype(BF16)
    queries = ((dot_n(normed, qw[...]) + qb[...]) * channels ** (-0.5)).astype(BF16)
    keys = dot_n(normed, kw[...]).astype(BF16)
    values = (dot_n(normed, vw[...]) + vb[...]).astype(BF16)
    scores = dot_t(queries, keys)
    query_frame = (lax.broadcasted_iota(jnp.int32, scores.shape, 0) // width) % 2
    key_frame = (lax.broadcasted_iota(jnp.int32, scores.shape, 1) // width) % 2
    allowed = query_frame >= key_frame
    scores = jnp.where(allowed, scores, NEGATIVE)
    top = jnp.max(scores, axis=1, keepdims=True)
    weights = jnp.where(allowed, jnp.exp(scores - top), 0.0)
    denominator = jnp.sum(weights, axis=1, keepdims=True)
    attended = (dot_n(weights.astype(BF16), values) / denominator).astype(BF16)
    mixed = (
        gath[...].reshape(tokens, channels).astype(F32) + dot_n(attended, ow[...]) + ob[...]
    )
    mixed = mixed.astype(BF16).astype(F32).reshape(count, 2, width, channels)
    shifted_inputs(mixed[:, 0], x0_ref)
    shifted_inputs(mixed[:, 1], x1_ref)

    outs = cw_ref.shape[1]
    lanes = 4 * outs
    bias_row = jnp.broadcast_to(cb[...], (8, channels))
    own = jnp.zeros((8, outs), F32)
    for k in range(count):
        own = jnp.where(me == k, bias_row[:, k * outs : (k + 1) * outs], own)
    bias = jnp.concatenate([own] * 4, axis=1)[:1]
    first = dot_t(x0_ref[...], w0_ref[...])
    second = dot_t(x1_ref[...], w1_ref[...])
    frames = [
        first[:, :lanes] + bias,
        first[:, lanes : 2 * lanes] + second[:, :lanes] + bias,
        first[:, 2 * lanes :] + second[:, lanes:] + bias,
    ]
    frames = [f.reshape(count, width, lanes) for f in frames]
    packed = jnp.concatenate(frames + [jnp.zeros_like(frames[0])], axis=1)
    sendbuf[...] = packed.astype(BF16)

    def out_copy(row, source, to, slot):
        return pltpu.make_async_remote_copy(
            src_ref=sendbuf.at[row],
            dst_ref=recvbuf.at[source],
            send_sem=osend_sem.at[slot],
            recv_sem=orecv_sem.at[source],
            device_id={"space": to},
            device_id_type=MESH,
        )

    for k in range(1, count):
        to = lax.rem(me + k, count)
        send = out_copy(to, me, to, k)
        send.start()
        sends.append(send)
    own_copy = pltpu.make_async_copy(sendbuf.at[me], recvbuf.at[me], osend_sem.at[0])
    own_copy.start()
    own_copy.wait()
    for k in range(1, count):
        source = lax.rem(me + count - k, count)
        out_copy(source, source, me, k).wait_recv()

    each = 128 // outs
    for j in range(count // each):
        parts = [recvbuf[j * each + i].astype(F32) for i in range(each)]
        for p in range(2):
            for q in range(2):
                at = (p * 2 + q) * outs
                joined = jnp.concatenate([part[:, at : at + outs] for part in parts], axis=1)
                for t in range(3):
                    base = (t * 2 + p) * 2 * width + q
                    wide[j, pl.ds(base, width, stride=2), :] = joined[t * width : (t + 1) * width]
    for j in range(count // each):
        out_ref[:, j * 128 : (j + 1) * 128] = wide[j].astype(BF16)
    for send in sends:
        send.wait_send()


def per_device_fused(
    features,
    norm_gain,
    norm_bias,
    query_weight,
    query_bias,
    key_weight,
    value_weight,
    value_bias,
    out_weight,
    out_bias,
    conv_weight,
    conv_bias,
):
    count = lax.axis_size("space")
    frames, _, width, channels = features.shape
    outs = conv_weight.shape[4]
    rows = count * width
    taps = jnp.swapaxes(conv_weight, 3, 4).reshape(27, outs, channels)
    vmem = pl.BlockSpec(memory_space=pltpu.VMEM)
    hbm = pl.BlockSpec(memory_space=pltpu.HBM)
    vector = pltpu.VMEM((1, channels), F32)
    square = pltpu.VMEM((channels, channels), BF16)
    row = lambda v: v.reshape(1, channels)
    out_rows = 3 * 2 * 2 * width
    decoded = pl.pallas_call(
        functools.partial(fused_kernel, count),
        out_shape=jax.ShapeDtypeStruct((out_rows, channels), BF16),
        in_specs=[hbm] * 12,
        out_specs=vmem,
        scratch_shapes=[
            pltpu.VMEM((count, frames * width, channels), BF16),
            square,
            square,
            square,
            square,
            pltpu.VMEM((27, outs, channels), BF16),
            vector,
            vector,
            vector,
            vector,
            vector,
            vector,
            pltpu.VMEM((12 * outs, 9 * channels), BF16),
            pltpu.VMEM((8 * outs, 9 * channels), BF16),
            pltpu.VMEM((rows, 9 * channels), BF16),
            pltpu.VMEM((rows, 9 * channels), BF16),
            pltpu.VMEM((count, 4 * width, 4 * outs), BF16),
            pltpu.VMEM((count, 4 * width, 4 * outs), BF16),
            pltpu.VMEM((channels // 128, out_rows, 128), F32),
            pltpu.SemaphoreType.DMA((12,)),
            pltpu.SemaphoreType.DMA((count,)),
            pltpu.SemaphoreType.DMA((count,)),
            pltpu.SemaphoreType.DMA((count,)),
            pltpu.SemaphoreType.DMA((count,)),
        ],
        compiler_params=pltpu.CompilerParams(
            collective_id=0, has_side_effects=True, vmem_limit_bytes=63 * 1024 * 1024
        ),
    )(
        features.reshape(frames * width, channels),
        row(norm_gain),
        row(norm_bias),
        query_weight,
        row(query_bias),
        key_weight,
        value_weight,
        row(value_bias),
        out_weight,
        row(out_bias),
        taps,
        row(conv_bias),
    )
    return decoded.reshape(3, 2, 2 * width, channels)


def per_device(features, *rest):
    count = lax.axis_size("space")
    frames, local_rows, width, channels = features.shape
    outs = rest[9].shape[4]
    if (frames, local_rows, width) == (2, 1, 8) and outs == 32 and count % 4 == 0:
        return per_device_fused(features, *rest)
    return per_device_sharded(features, *rest)


def solution(mesh):
    placed = (
        P("groups", "space", None, None),
        P(),
        P(),
        P(),
        P(),
        P(),
        P(),
        P(),
        P(),
        P(),
        P(None, None, None, None, "space"),
        P(),
    )
    return jax.shard_map(
        per_device,
        mesh=mesh,
        in_specs=placed,
        out_specs=P("groups", "space", None, None),
        check_vma=False,
    )
```

```python
import functools

import jax
import jax.numpy as jnp
from jax import lax
from jax.experimental import pallas as pl
from jax.experimental.pallas import tpu as pltpu
from jax.sharding import PartitionSpec as P

GROUPS = 32


EPSILON = 1e-06
NEGATIVE = -1e30


def with_halo(value, sides, width):
    for axis, dim in sides:
        count, length = (lax.axis_size(axis), value.shape[dim])
        up = [(i, (i + 1) % count) for i in range(count - 1)]
        down = [(j, i) for i, j in up]
        last = lax.slice_in_dim(value, length - width, length, axis=dim)
        leading = lax.slice_in_dim(value, 0, width, axis=dim)
        before = lax.ppermute(last, axis, up)
        after = lax.ppermute(leading, axis, down)
        value = jnp.concatenate([before, value, after], axis=dim)
    return value


def upsample_conv(row_band, weight):
    repeated = jnp.repeat(row_band[1:], 2, axis=0)
    frames = jnp.concatenate([row_band[:1], repeated], axis=0)
    doubled_rows = jnp.repeat(frames, 2, axis=1)[:, 1:-1]
    columns = jnp.repeat(doubled_rows, 2, axis=2)
    columns = jnp.concatenate([columns[:, :, :1], columns, columns[:, :, -1:]], axis=2)
    padded = jnp.concatenate([columns[:1], columns[:1], columns], axis=0)
    out_frames = frames.shape[0]
    out_rows = doubled_rows.shape[1] - 2
    out_cols = columns.shape[2] - 2
    channels = row_band.shape[3]
    out_width = weight.shape[4]
    result = jnp.zeros((out_frames * out_rows * out_cols, out_width), jnp.float32)
    for time_tap in range(3):
        for row_tap in range(3):
            for col_tap in range(3):
                window = padded[
                    time_tap : time_tap + out_frames,
                    row_tap : row_tap + out_rows,
                    col_tap : col_tap + out_cols,
                ]
                result = result + jnp.dot(
                    window.reshape(-1, channels),
                    weight[time_tap, row_tap, col_tap],
                    preferred_element_type=jnp.float32,
                )
    return result.reshape(out_frames, out_rows, out_cols, out_width)


def per_device_sharded(
    features,
    norm_gain,
    norm_bias,
    query_weight,
    query_bias,
    key_weight,
    value_weight,
    value_bias,
    out_weight,
    out_bias,
    conv_weight,
    conv_bias,
):
    frames, local_rows, columns, channels = features.shape
    spread = lax.axis_size("space")
    grouped = features.astype(jnp.float32).reshape(-1, GROUPS, channels // GROUPS)
    entries = grouped.shape[0] * grouped.shape[2] * spread
    group_mean = lax.psum(jnp.sum(grouped, axis=(0, 2)), "space") / entries
    centred = grouped - group_mean[None, :, None]
    variance = lax.psum(jnp.sum(centred * centred, axis=(0, 2)), "space") / entries
    normed = (
        (centred * lax.rsqrt(variance + EPSILON)[None, :, None]).reshape(-1, channels) * norm_gain
        + norm_bias
    ).astype(jnp.bfloat16)
    softmax_scale = channels ** (-0.5)
    queries = (
        (jnp.dot(normed, query_weight, preferred_element_type=jnp.float32) + query_bias)
        * softmax_scale
    ).astype(jnp.bfloat16)
    key_tiles = (
        jnp.dot(normed, key_weight, preferred_element_type=jnp.float32)
        .astype(jnp.bfloat16)
        .reshape(frames, local_rows, columns, channels)
    )
    value_tiles = (
        (jnp.dot(normed, value_weight, preferred_element_type=jnp.float32) + value_bias)
        .astype(jnp.bfloat16)
        .reshape(frames, local_rows, columns, channels)
    )
    local_count = queries.shape[0]
    query_frame = jnp.arange(local_count) // (local_rows * columns)
    running_max = jnp.full((local_count,), NEGATIVE, jnp.float32)
    key_piece = lax.all_gather(key_tiles, "space", axis=1, tiled=True)
    value_piece = lax.all_gather(value_tiles, "space", axis=1, tiled=True)
    per_frame = key_piece.shape[1] * key_piece.shape[2]
    key_rows = key_piece.reshape(-1, channels)
    value_rows = value_piece.reshape(-1, channels)
    key_frame = jnp.arange(key_rows.shape[0]) // per_frame
    allowed = query_frame[:, None] >= key_frame[None, :]
    scores = jnp.where(
        allowed, jnp.dot(queries, key_rows.T, preferred_element_type=jnp.float32), NEGATIVE
    )
    new_max = jnp.maximum(running_max, jnp.max(scores, axis=1))
    weights = jnp.where(allowed, jnp.exp(scores - new_max[:, None]), 0.0)
    denominator = jnp.sum(weights, axis=1)
    weighted = jnp.dot(weights.astype(jnp.bfloat16), value_rows, preferred_element_type=jnp.float32)
    running_max, denominator, weighted = (new_max, denominator, weighted)
    attended = (weighted / denominator[:, None]).astype(jnp.bfloat16)
    mixed_tokens = (
        features.reshape(-1, channels).astype(jnp.float32)
        + jnp.dot(attended, out_weight, preferred_element_type=jnp.float32)
        + out_bias
    ).astype(jnp.bfloat16)
    mixed_tokens = mixed_tokens.reshape(frames, local_rows, columns, channels)
    rimmed = with_halo(mixed_tokens, (("space", 1),), 1)
    position = lax.axis_index("space")
    upper_rim = jnp.where(position == 0, mixed_tokens, rimmed[:, :1])
    lower_rim = jnp.where(position == spread - 1, mixed_tokens, rimmed[:, -1:])
    row_band = jnp.concatenate([upper_rim, mixed_tokens, lower_rim], axis=1)
    convolved = upsample_conv(row_band, lax.all_gather(conv_weight, "space", axis=4, tiled=True))
    decoded = (convolved + conv_bias).astype(jnp.bfloat16)
    return decoded


MESH = pl.DeviceIdType.MESH
F32 = jnp.float32
BF16 = jnp.bfloat16


def dot_t(a, b):
    return lax.dot_general(a, b, (((1,), (1,)), ((), ())), preferred_element_type=F32)


def dot_n(a, b):
    return jnp.dot(a, b, preferred_element_type=F32)


def group_total(row, width):
    channels = row.shape[1]
    lane = lax.broadcasted_iota(jnp.int32, row.shape, 1)
    step = 1
    while step < width:
        high = (lane // step) % 2 == 1
        row = row + jnp.where(
            high, pltpu.roll(row, step, 1), pltpu.roll(row, channels - step, 1)
        )
        step *= 2
    return row


def fold_conv_weights(conv_v, w0_ref, w1_ref):
    outs, channels = conv_v.shape[1], conv_v.shape[2]
    zero = jnp.zeros((outs, channels), BF16)
    combos = (
        (w0_ref, 0, (0, 1, 2)),
        (w0_ref, 1, (0, 1)),
        (w0_ref, 2, (0,)),
        (w1_ref, 0, (2,)),
        (w1_ref, 1, (1, 2)),
    )
    spatial = {
        (0, 0): (0,),
        (0, 1): (1, 2),
        (1, 1): (0, 1),
        (1, 2): (2,),
    }
    for ref, slot, times in combos:
        summed = {}
        for b in range(3):
            for e in range(3):
                value = conv_v[times[0] * 9 + b * 3 + e].astype(F32)
                for a in times[1:]:
                    value = value + conv_v[a * 9 + b * 3 + e].astype(F32)
                summed[b, e] = value
        for p in range(2):
            for dr in range(3):
                rows = spatial.get((p, dr))
                if rows is not None:
                    by_col = []
                    for e in range(3):
                        value = summed[rows[0], e]
                        for b in rows[1:]:
                            value = value + summed[b, e]
                        by_col.append(value)
                for q in range(2):
                    for dc in range(3):
                        cols = spatial.get((q, dc))
                        if rows is None or cols is None:
                            piece = zero
                        else:
                            value = by_col[cols[0]]
                            for e in cols[1:]:
                                value = value + by_col[e]
                            piece = value.astype(BF16)
                        at = slot * 4 * outs + (p * 2 + q) * outs
                        tap = (dr * 3 + dc) * channels
                        ref[at : at + outs, tap : tap + channels] = piece


def shifted_inputs(frame, x_ref):
    height, width, channels = frame.shape
    column = lax.broadcasted_iota(jnp.int32, frame.shape, 1)
    left = jnp.where(column == 0, frame, jnp.roll(frame, 1, axis=1))
    right = jnp.where(column == width - 1, frame, jnp.roll(frame, -1, axis=1))
    for dc, plane in enumerate((left, frame, right)):
        up = jnp.concatenate([plane[:1], plane[:-1]], axis=0)
        down = jnp.concatenate([plane[1:], plane[-1:]], axis=0)
        for dr, moved in enumerate((up, plane, down)):
            tap = (dr * 3 + dc) * channels
            x_ref[:, tap : tap + channels] = moved.reshape(height * width, channels).astype(BF16)


def fused_kernel(
    count,
    feat_ref,
    gain_ref,
    nbias_ref,
    qw_ref,
    qb_ref,
    kw_ref,
    vw_ref,
    vb_ref,
    ow_ref,
    ob_ref,
    cw_ref,
    cb_ref,
    out_ref,
    gath,
    qw,
    kw,
    vw,
    ow,
    cw,
    gain,
    nbias,
    qb,
    vb,
    ob,
    cb,
    w0_ref,
    w1_ref,
    x0_ref,
    x1_ref,
    sendbuf,
    recvbuf,
    wide,
    load_sem,
    fsend_sem,
    frecv_sem,
    osend_sem,
    orecv_sem,
):
    me = lax.axis_index("space")
    chips = count // 2
    sibling = me + 1 - 2 * lax.rem(me, 2)
    width, channels = feat_ref.shape[0] // 2, feat_ref.shape[1]

    barrier = pltpu.get_barrier_semaphore()
    for k in range(1, count):
        pl.semaphore_signal(
            barrier, inc=1, device_id={"space": lax.rem(me + k, count)}, device_id_type=MESH
        )
    loads = [
        pltpu.make_async_copy(s, d, load_sem.at[i])
        for i, (s, d) in enumerate(
            (
                (feat_ref, gath.at[me]),
                (cw_ref, cw),
                (gain_ref, gain),
                (nbias_ref, nbias),
                (qw_ref, qw),
                (kw_ref, kw),
                (vw_ref, vw),
                (ow_ref, ow),
                (qb_ref, qb),
                (vb_ref, vb),
                (ob_ref, ob),
                (cb_ref, cb),
            )
        )
    ]
    for load in loads:
        load.start()
    pl.semaphore_wait(barrier, count - 1)

    sends = []
    def feat_copy(src, block, to, slot):
        return pltpu.make_async_remote_copy(
            src_ref=src,
            dst_ref=gath.at[block],
            send_sem=fsend_sem.at[slot],
            recv_sem=frecv_sem.at[block],
            device_id={"space": to},
            device_id_type=MESH,
        )

    sends = [
        feat_copy(feat_ref, me, lax.rem(me + 2 * k, count), k) for k in range(1, chips)
    ] + [feat_copy(feat_ref, me, sibling, 0)]
    for send in sends:
        send.start()

    loads[1].wait()
    fold_conv_weights(cw, w0_ref, w1_ref)

    for k in range(1, chips):
        block = lax.rem(me + count - 2 * k, count)
        feat_copy(feat_ref, block, sibling, 0).wait_recv()
        forward = feat_copy(gath.at[block], block, sibling, chips + k)
        forward.start()
        sends.append(forward)
    for load in loads[2:]:
        load.wait()
    loads[0].wait()
    for k in range(chips):
        block = lax.rem(sibling + count - 2 * k, count)
        feat_copy(feat_ref, block, sibling, 0).wait_recv()

    tokens = count * 2 * width
    feats = gath[...].reshape(tokens, channels).astype(F32)
    group_width = channels // GROUPS
    entries = tokens * group_width
    column = jnp.broadcast_to(jnp.sum(feats, axis=0, keepdims=True), (8, channels))
    mean = group_total(column, group_width)[:1] / entries
    centred = feats - mean
    column = jnp.broadcast_to(jnp.sum(centred * centred, axis=0, keepdims=True), (8, channels))
    variance = group_total(column, group_width)[:1] / entries
    normed = (centred * lax.rsqrt(variance + EPSILON) * gain[...] + nbias[...]).astype(BF16)
    queries = ((dot_n(normed, qw[...]) + qb[...]) * channels ** (-0.5)).astype(BF16)
    keys = dot_n(normed, kw[...]).astype(BF16)
    values = (dot_n(normed, vw[...]) + vb[...]).astype(BF16)
    scores = dot_t(queries, keys)
    query_frame = (lax.broadcasted_iota(jnp.int32, scores.shape, 0) // width) % 2
    key_frame = (lax.broadcasted_iota(jnp.int32, scores.shape, 1) // width) % 2
    allowed = query_frame >= key_frame
    scores = jnp.where(allowed, scores, NEGATIVE)
    top = jnp.max(scores, axis=1, keepdims=True)
    weights = jnp.where(allowed, jnp.exp(scores - top), 0.0)
    denominator = jnp.sum(weights, axis=1, keepdims=True)
    attended = (dot_n(weights.astype(BF16), values) / denominator).astype(BF16)
    mixed = (
        gath[...].reshape(tokens, channels).astype(F32) + dot_n(attended, ow[...]) + ob[...]
    )
    mixed = mixed.astype(BF16).astype(F32).reshape(count, 2, width, channels)
    shifted_inputs(mixed[:, 0], x0_ref)
    shifted_inputs(mixed[:, 1], x1_ref)

    outs = cw_ref.shape[1]
    lanes = 4 * outs
    bias_row = jnp.broadcast_to(cb[...], (8, channels))
    own = jnp.zeros((8, outs), F32)
    for k in range(count):
        own = jnp.where(me == k, bias_row[:, k * outs : (k + 1) * outs], own)
    bias = jnp.concatenate([own] * 4, axis=1)[:1]
    first = dot_t(x0_ref[...], w0_ref[...])
    second = dot_t(x1_ref[...], w1_ref[...])
    frames = [
        first[:, :lanes] + bias,
        first[:, lanes : 2 * lanes] + second[:, :lanes] + bias,
        first[:, 2 * lanes :] + second[:, lanes:] + bias,
    ]
    frames = [f.reshape(count, width, lanes) for f in frames]
    packed = jnp.concatenate(frames + [jnp.zeros_like(frames[0])], axis=1)
    sendbuf[...] = packed.astype(BF16)

    def out_copy(row, source, to, slot):
        return pltpu.make_async_remote_copy(
            src_ref=sendbuf.at[row],
            dst_ref=recvbuf.at[source],
            send_sem=osend_sem.at[slot],
            recv_sem=orecv_sem.at[source],
            device_id={"space": to},
            device_id_type=MESH,
        )

    for k in range(1, count):
        to = lax.rem(me + k, count)
        send = out_copy(to, me, to, k)
        send.start()
        sends.append(send)
    own_copy = pltpu.make_async_copy(sendbuf.at[me], recvbuf.at[me], osend_sem.at[0])
    own_copy.start()
    own_copy.wait()
    for k in range(1, count):
        source = lax.rem(me + count - k, count)
        out_copy(source, source, me, k).wait_recv()

    each = 128 // outs
    for j in range(count // each):
        parts = [recvbuf[j * each + i].astype(F32) for i in range(each)]
        for p in range(2):
            for q in range(2):
                at = (p * 2 + q) * outs
                joined = jnp.concatenate([part[:, at : at + outs] for part in parts], axis=1)
                for t in range(3):
                    base = (t * 2 + p) * 2 * width + q
                    wide[j, pl.ds(base, width, stride=2), :] = joined[t * width : (t + 1) * width]
    for j in range(count // each):
        out_ref[:, j * 128 : (j + 1) * 128] = wide[j].astype(BF16)
    for send in sends:
        send.wait_send()


def per_device_fused(
    features,
    norm_gain,
    norm_bias,
    query_weight,
    query_bias,
    key_weight,
    value_weight,
    value_bias,
    out_weight,
    out_bias,
    conv_weight,
    conv_bias,
):
    count = lax.axis_size("space")
    frames, _, width, channels = features.shape
    outs = conv_weight.shape[4]
    rows = count * width
    taps = jnp.swapaxes(conv_weight, 3, 4).reshape(27, outs, channels)
    vmem = pl.BlockSpec(memory_space=pltpu.VMEM)
    hbm = pl.BlockSpec(memory_space=pltpu.HBM)
    vector = pltpu.VMEM((1, channels), F32)
    square = pltpu.VMEM((channels, channels), BF16)
    row = lambda v: v.reshape(1, channels)
    out_rows = 3 * 2 * 2 * width
    decoded = pl.pallas_call(
        functools.partial(fused_kernel, count),
        out_shape=pltpu.VMEM((out_rows, channels), BF16),
        in_specs=[hbm] * 12,
        out_specs=vmem,
        scratch_shapes=[
            pltpu.VMEM((count, frames * width, channels), BF16),
            square,
            square,
            square,
            square,
            pltpu.VMEM((27, outs, channels), BF16),
            vector,
            vector,
            vector,
            vector,
            vector,
            vector,
            pltpu.VMEM((12 * outs, 9 * channels), BF16),
            pltpu.VMEM((8 * outs, 9 * channels), BF16),
            pltpu.VMEM((rows, 9 * channels), BF16),
            pltpu.VMEM((rows, 9 * channels), BF16),
            pltpu.VMEM((count, 4 * width, 4 * outs), BF16),
            pltpu.VMEM((count, 4 * width, 4 * outs), BF16),
            pltpu.VMEM((channels // 128, out_rows, 128), F32),
            pltpu.SemaphoreType.DMA((12,)),
            pltpu.SemaphoreType.DMA((count,)),
            pltpu.SemaphoreType.DMA((count,)),
            pltpu.SemaphoreType.DMA((count,)),
            pltpu.SemaphoreType.DMA((count,)),
        ],
        compiler_params=pltpu.CompilerParams(
            collective_id=0, has_side_effects=True, vmem_limit_bytes=44 * 1024 * 1024
        ),
    )(
        *(
            pltpu.with_memory_space_constraint(operand, pltpu.HBM)
            for operand in (
                features.reshape(frames * width, channels),
                row(norm_gain),
                row(norm_bias),
                query_weight,
                row(query_bias),
                key_weight,
                value_weight,
                row(value_bias),
                out_weight,
                row(out_bias),
                taps,
                row(conv_bias),
            )
        )
    )
    return decoded.reshape(3, 2, 2 * width, channels)


def per_device(features, *rest):
    count = lax.axis_size("space")
    frames, local_rows, width, channels = features.shape
    outs = rest[9].shape[4]
    if (frames, local_rows, width) == (2, 1, 8) and outs == 32 and count % 4 == 0:
        return per_device_fused(features, *rest)
    return per_device_sharded(features, *rest)


def solution(mesh):
    placed = (
        P("groups", "space", None, None),
        P(),
        P(),
        P(),
        P(),
        P(),
        P(),
        P(),
        P(),
        P(),
        P(None, None, None, None, "space"),
        P(),
    )
    return jax.shard_map(
        per_device,
        mesh=mesh,
        in_specs=placed,
        out_specs=P("groups", "space", None, None),
        check_vma=False,
    )
```

```python
import functools

import jax
import jax.numpy as jnp
from jax import lax
from jax.experimental import pallas as pl
from jax.experimental.pallas import tpu as pltpu
from jax.sharding import PartitionSpec as P

GROUPS = 32


EPSILON = 1e-06
NEGATIVE = -1e30


def with_halo(value, sides, width):
    for axis, dim in sides:
        count, length = (lax.axis_size(axis), value.shape[dim])
        up = [(i, (i + 1) % count) for i in range(count - 1)]
        down = [(j, i) for i, j in up]
        last = lax.slice_in_dim(value, length - width, length, axis=dim)
        leading = lax.slice_in_dim(value, 0, width, axis=dim)
        before = lax.ppermute(last, axis, up)
        after = lax.ppermute(leading, axis, down)
        value = jnp.concatenate([before, value, after], axis=dim)
    return value


def upsample_conv(row_band, weight):
    repeated = jnp.repeat(row_band[1:], 2, axis=0)
    frames = jnp.concatenate([row_band[:1], repeated], axis=0)
    doubled_rows = jnp.repeat(frames, 2, axis=1)[:, 1:-1]
    columns = jnp.repeat(doubled_rows, 2, axis=2)
    columns = jnp.concatenate([columns[:, :, :1], columns, columns[:, :, -1:]], axis=2)
    padded = jnp.concatenate([columns[:1], columns[:1], columns], axis=0)
    out_frames = frames.shape[0]
    out_rows = doubled_rows.shape[1] - 2
    out_cols = columns.shape[2] - 2
    channels = row_band.shape[3]
    out_width = weight.shape[4]
    result = jnp.zeros((out_frames * out_rows * out_cols, out_width), jnp.float32)
    for time_tap in range(3):
        for row_tap in range(3):
            for col_tap in range(3):
                window = padded[
                    time_tap : time_tap + out_frames,
                    row_tap : row_tap + out_rows,
                    col_tap : col_tap + out_cols,
                ]
                result = result + jnp.dot(
                    window.reshape(-1, channels),
                    weight[time_tap, row_tap, col_tap],
                    preferred_element_type=jnp.float32,
                )
    return result.reshape(out_frames, out_rows, out_cols, out_width)


def per_device_sharded(
    features,
    norm_gain,
    norm_bias,
    query_weight,
    query_bias,
    key_weight,
    value_weight,
    value_bias,
    out_weight,
    out_bias,
    conv_weight,
    conv_bias,
):
    frames, local_rows, columns, channels = features.shape
    spread = lax.axis_size("space")
    grouped = features.astype(jnp.float32).reshape(-1, GROUPS, channels // GROUPS)
    entries = grouped.shape[0] * grouped.shape[2] * spread
    group_mean = lax.psum(jnp.sum(grouped, axis=(0, 2)), "space") / entries
    centred = grouped - group_mean[None, :, None]
    variance = lax.psum(jnp.sum(centred * centred, axis=(0, 2)), "space") / entries
    normed = (
        (centred * lax.rsqrt(variance + EPSILON)[None, :, None]).reshape(-1, channels) * norm_gain
        + norm_bias
    ).astype(jnp.bfloat16)
    softmax_scale = channels ** (-0.5)
    queries = (
        (jnp.dot(normed, query_weight, preferred_element_type=jnp.float32) + query_bias)
        * softmax_scale
    ).astype(jnp.bfloat16)
    key_tiles = (
        jnp.dot(normed, key_weight, preferred_element_type=jnp.float32)
        .astype(jnp.bfloat16)
        .reshape(frames, local_rows, columns, channels)
    )
    value_tiles = (
        (jnp.dot(normed, value_weight, preferred_element_type=jnp.float32) + value_bias)
        .astype(jnp.bfloat16)
        .reshape(frames, local_rows, columns, channels)
    )
    local_count = queries.shape[0]
    query_frame = jnp.arange(local_count) // (local_rows * columns)
    running_max = jnp.full((local_count,), NEGATIVE, jnp.float32)
    key_piece = lax.all_gather(key_tiles, "space", axis=1, tiled=True)
    value_piece = lax.all_gather(value_tiles, "space", axis=1, tiled=True)
    per_frame = key_piece.shape[1] * key_piece.shape[2]
    key_rows = key_piece.reshape(-1, channels)
    value_rows = value_piece.reshape(-1, channels)
    key_frame = jnp.arange(key_rows.shape[0]) // per_frame
    allowed = query_frame[:, None] >= key_frame[None, :]
    scores = jnp.where(
        allowed, jnp.dot(queries, key_rows.T, preferred_element_type=jnp.float32), NEGATIVE
    )
    new_max = jnp.maximum(running_max, jnp.max(scores, axis=1))
    weights = jnp.where(allowed, jnp.exp(scores - new_max[:, None]), 0.0)
    denominator = jnp.sum(weights, axis=1)
    weighted = jnp.dot(weights.astype(jnp.bfloat16), value_rows, preferred_element_type=jnp.float32)
    running_max, denominator, weighted = (new_max, denominator, weighted)
    attended = (weighted / denominator[:, None]).astype(jnp.bfloat16)
    mixed_tokens = (
        features.reshape(-1, channels).astype(jnp.float32)
        + jnp.dot(attended, out_weight, preferred_element_type=jnp.float32)
        + out_bias
    ).astype(jnp.bfloat16)
    mixed_tokens = mixed_tokens.reshape(frames, local_rows, columns, channels)
    rimmed = with_halo(mixed_tokens, (("space", 1),), 1)
    position = lax.axis_index("space")
    upper_rim = jnp.where(position == 0, mixed_tokens, rimmed[:, :1])
    lower_rim = jnp.where(position == spread - 1, mixed_tokens, rimmed[:, -1:])
    row_band = jnp.concatenate([upper_rim, mixed_tokens, lower_rim], axis=1)
    convolved = upsample_conv(row_band, lax.all_gather(conv_weight, "space", axis=4, tiled=True))
    decoded = (convolved + conv_bias).astype(jnp.bfloat16)
    return decoded


MESH = pl.DeviceIdType.MESH
F32 = jnp.float32
BF16 = jnp.bfloat16


def dot_t(a, b):
    return lax.dot_general(a, b, (((1,), (1,)), ((), ())), preferred_element_type=F32)


def dot_n(a, b):
    return jnp.dot(a, b, preferred_element_type=F32)


def group_total(row, width):
    channels = row.shape[1]
    lane = lax.broadcasted_iota(jnp.int32, row.shape, 1)
    step = 1
    while step < width:
        high = (lane // step) % 2 == 1
        row = row + jnp.where(
            high, pltpu.roll(row, step, 1), pltpu.roll(row, channels - step, 1)
        )
        step *= 2
    return row


def fold_conv_weights(conv_v, w0_ref, w1_ref):
    outs, channels = conv_v.shape[1], conv_v.shape[2]
    zero = jnp.zeros((outs, channels), BF16)
    combos = (
        (w0_ref, 0, (0, 1, 2)),
        (w0_ref, 1, (0, 1)),
        (w0_ref, 2, (0,)),
        (w1_ref, 0, (2,)),
        (w1_ref, 1, (1, 2)),
    )
    spatial = {
        (0, 0): (0,),
        (0, 1): (1, 2),
        (1, 1): (0, 1),
        (1, 2): (2,),
    }
    for ref, slot, times in combos:
        summed = {}
        for b in range(3):
            for e in range(3):
                value = conv_v[times[0] * 9 + b * 3 + e].astype(F32)
                for a in times[1:]:
                    value = value + conv_v[a * 9 + b * 3 + e].astype(F32)
                summed[b, e] = value
        for p in range(2):
            for dr in range(3):
                rows = spatial.get((p, dr))
                if rows is not None:
                    by_col = []
                    for e in range(3):
                        value = summed[rows[0], e]
                        for b in rows[1:]:
                            value = value + summed[b, e]
                        by_col.append(value)
                for q in range(2):
                    for dc in range(3):
                        cols = spatial.get((q, dc))
                        if rows is None or cols is None:
                            piece = zero
                        else:
                            value = by_col[cols[0]]
                            for e in cols[1:]:
                                value = value + by_col[e]
                            piece = value.astype(BF16)
                        at = slot * 4 * outs + (p * 2 + q) * outs
                        tap = (dr * 3 + dc) * channels
                        ref[at : at + outs, tap : tap + channels] = piece


def shifted_inputs(frame, x_ref):
    height, width, channels = frame.shape
    column = lax.broadcasted_iota(jnp.int32, frame.shape, 1)
    left = jnp.where(column == 0, frame, jnp.roll(frame, 1, axis=1))
    right = jnp.where(column == width - 1, frame, jnp.roll(frame, -1, axis=1))
    for dc, plane in enumerate((left, frame, right)):
        up = jnp.concatenate([plane[:1], plane[:-1]], axis=0)
        down = jnp.concatenate([plane[1:], plane[-1:]], axis=0)
        for dr, moved in enumerate((up, plane, down)):
            tap = (dr * 3 + dc) * channels
            x_ref[:, tap : tap + channels] = moved.reshape(height * width, channels).astype(BF16)


def fused_kernel(
    count,
    feat_ref,
    gain_ref,
    nbias_ref,
    qw_ref,
    qb_ref,
    kw_ref,
    vw_ref,
    vb_ref,
    ow_ref,
    ob_ref,
    cw_ref,
    cb_ref,
    out_ref,
    gath,
    qw,
    kw,
    vw,
    ow,
    cw,
    gain,
    nbias,
    qb,
    vb,
    ob,
    cb,
    w0_ref,
    w1_ref,
    x0_ref,
    x1_ref,
    sendbuf,
    recvbuf,
    wide,
    load_sem,
    fsend_sem,
    frecv_sem,
    osend_sem,
    orecv_sem,
):
    me = lax.axis_index("space")
    chips = count // 2
    sibling = me + 1 - 2 * lax.rem(me, 2)
    width, channels = feat_ref.shape[0] // 2, feat_ref.shape[1]

    barrier = pltpu.get_barrier_semaphore()
    for k in range(1, count):
        pl.semaphore_signal(
            barrier, inc=1, device_id={"space": lax.rem(me + k, count)}, device_id_type=MESH
        )
    loads = [
        pltpu.make_async_copy(s, d, load_sem.at[i])
        for i, (s, d) in enumerate(
            (
                (feat_ref, gath.at[me]),
                (cw_ref, cw),
                (gain_ref, gain),
                (nbias_ref, nbias),
                (qw_ref, qw),
                (kw_ref, kw),
                (vw_ref, vw),
                (ow_ref, ow),
                (qb_ref, qb),
                (vb_ref, vb),
                (ob_ref, ob),
                (cb_ref, cb),
            )
        )
    ]
    for load in loads:
        load.start()
    pl.semaphore_wait(barrier, count - 1)

    sends = []
    def feat_copy(src, block, to, slot):
        return pltpu.make_async_remote_copy(
            src_ref=src,
            dst_ref=gath.at[block],
            send_sem=fsend_sem.at[slot],
            recv_sem=frecv_sem.at[block],
            device_id={"space": to},
            device_id_type=MESH,
        )

    sends = [
        feat_copy(feat_ref, me, lax.rem(me + 2 * k, count), k) for k in range(1, chips)
    ] + [feat_copy(feat_ref, me, sibling, 0)]
    for send in sends:
        send.start()

    loads[1].wait()
    fold_conv_weights(cw, w0_ref, w1_ref)

    for k in range(1, chips):
        block = lax.rem(me + count - 2 * k, count)
        feat_copy(feat_ref, block, sibling, 0).wait_recv()
        forward = feat_copy(gath.at[block], block, sibling, chips + k)
        forward.start()
        sends.append(forward)
    for load in loads[2:]:
        load.wait()
    loads[0].wait()
    for k in range(chips):
        block = lax.rem(sibling + count - 2 * k, count)
        feat_copy(feat_ref, block, sibling, 0).wait_recv()

    tokens = count * 2 * width
    feats = gath[...].reshape(tokens, channels).astype(F32)
    group_width = channels // GROUPS
    entries = tokens * group_width
    column = jnp.broadcast_to(jnp.sum(feats, axis=0, keepdims=True), (8, channels))
    mean = group_total(column, group_width)[:1] / entries
    centred = feats - mean
    column = jnp.broadcast_to(jnp.sum(centred * centred, axis=0, keepdims=True), (8, channels))
    variance = group_total(column, group_width)[:1] / entries
    normed = (centred * lax.rsqrt(variance + EPSILON) * gain[...] + nbias[...]).astype(BF16)
    queries = ((dot_n(normed, qw[...]) + qb[...]) * channels ** (-0.5)).astype(BF16)
    keys = dot_n(normed, kw[...]).astype(BF16)
    values = (dot_n(normed, vw[...]) + vb[...]).astype(BF16)
    scores = dot_t(queries, keys)
    query_frame = (lax.broadcasted_iota(jnp.int32, scores.shape, 0) // width) % 2
    key_frame = (lax.broadcasted_iota(jnp.int32, scores.shape, 1) // width) % 2
    allowed = query_frame >= key_frame
    scores = jnp.where(allowed, scores, NEGATIVE)
    top = jnp.max(scores, axis=1, keepdims=True)
    weights = jnp.where(allowed, jnp.exp(scores - top), 0.0)
    denominator = jnp.sum(weights, axis=1, keepdims=True)
    attended = (dot_n(weights.astype(BF16), values) / denominator).astype(BF16)
    mixed = (
        gath[...].reshape(tokens, channels).astype(F32) + dot_n(attended, ow[...]) + ob[...]
    )
    mixed = mixed.astype(BF16).astype(F32).reshape(count, 2, width, channels)
    shifted_inputs(mixed[:, 0], x0_ref)
    shifted_inputs(mixed[:, 1], x1_ref)

    outs = cw_ref.shape[1]
    lanes = 4 * outs
    bias_row = jnp.broadcast_to(cb[...], (8, channels))
    own = jnp.zeros((8, outs), F32)
    for k in range(count):
        own = jnp.where(me == k, bias_row[:, k * outs : (k + 1) * outs], own)
    bias = jnp.concatenate([own] * 4, axis=1)[:1]
    first = dot_t(x0_ref[...], w0_ref[...])
    second = dot_t(x1_ref[...], w1_ref[...])
    frames = [
        first[:, :lanes] + bias,
        first[:, lanes : 2 * lanes] + second[:, :lanes] + bias,
        first[:, 2 * lanes :] + second[:, lanes:] + bias,
    ]
    frames = [f.reshape(count, width, lanes) for f in frames]
    packed = jnp.concatenate(frames + [jnp.zeros_like(frames[0])], axis=1)
    sendbuf[...] = packed.astype(BF16)

    def out_copy(row, source, to, slot):
        return pltpu.make_async_remote_copy(
            src_ref=sendbuf.at[row],
            dst_ref=recvbuf.at[source],
            send_sem=osend_sem.at[slot],
            recv_sem=orecv_sem.at[source],
            device_id={"space": to},
            device_id_type=MESH,
        )

    for k in range(1, count):
        to = lax.rem(me + k, count)
        send = out_copy(to, me, to, k)
        send.start()
        sends.append(send)
    own_copy = pltpu.make_async_copy(sendbuf.at[me], recvbuf.at[me], osend_sem.at[0])
    own_copy.start()

    each = 128 // outs
    blocks = count // each
    for step in range(blocks):
        j = lax.rem(me // each + step, blocks)
        first_source = j * each
        if step == 0:
            own_copy.wait()
            for m in range(1, each):
                source = first_source + lax.rem(me + m, each)
                out_copy(source, source, me, m).wait_recv()
        else:
            for m in range(each):
                source = first_source + m
                out_copy(source, source, me, 1).wait_recv()
        parts = [recvbuf[first_source + i].astype(F32) for i in range(each)]
        for p in range(2):
            for q in range(2):
                at = (p * 2 + q) * outs
                joined = jnp.concatenate([part[:, at : at + outs] for part in parts], axis=1)
                for t in range(3):
                    base = (t * 2 + p) * 2 * width + q
                    wide[j, pl.ds(base, width, stride=2), :] = joined[t * width : (t + 1) * width]
    for j in range(count // each):
        out_ref[:, j * 128 : (j + 1) * 128] = wide[j].astype(BF16)
    for send in sends:
        send.wait_send()


def per_device_fused(
    features,
    norm_gain,
    norm_bias,
    query_weight,
    query_bias,
    key_weight,
    value_weight,
    value_bias,
    out_weight,
    out_bias,
    conv_weight,
    conv_bias,
):
    count = lax.axis_size("space")
    frames, _, width, channels = features.shape
    outs = conv_weight.shape[4]
    rows = count * width
    taps = jnp.swapaxes(conv_weight, 3, 4).reshape(27, outs, channels)
    vmem = pl.BlockSpec(memory_space=pltpu.VMEM)
    hbm = pl.BlockSpec(memory_space=pltpu.HBM)
    vector = pltpu.VMEM((1, channels), F32)
    square = pltpu.VMEM((channels, channels), BF16)
    row = lambda v: v.reshape(1, channels)
    out_rows = 3 * 2 * 2 * width
    decoded = pl.pallas_call(
        functools.partial(fused_kernel, count),
        out_shape=pltpu.VMEM((out_rows, channels), BF16),
        in_specs=[hbm] * 12,
        out_specs=vmem,
        scratch_shapes=[
            pltpu.VMEM((count, frames * width, channels), BF16),
            square,
            square,
            square,
            square,
            pltpu.VMEM((27, outs, channels), BF16),
            vector,
            vector,
            vector,
            vector,
            vector,
            vector,
            pltpu.VMEM((12 * outs, 9 * channels), BF16),
            pltpu.VMEM((8 * outs, 9 * channels), BF16),
            pltpu.VMEM((rows, 9 * channels), BF16),
            pltpu.VMEM((rows, 9 * channels), BF16),
            pltpu.VMEM((count, 4 * width, 4 * outs), BF16),
            pltpu.VMEM((count, 4 * width, 4 * outs), BF16),
            pltpu.VMEM((channels // 128, out_rows, 128), F32),
            pltpu.SemaphoreType.DMA((12,)),
            pltpu.SemaphoreType.DMA((count,)),
            pltpu.SemaphoreType.DMA((count,)),
            pltpu.SemaphoreType.DMA((count,)),
            pltpu.SemaphoreType.DMA((count,)),
        ],
        compiler_params=pltpu.CompilerParams(
            collective_id=0, has_side_effects=True, vmem_limit_bytes=44 * 1024 * 1024
        ),
    )(
        *(
            pltpu.with_memory_space_constraint(operand, pltpu.HBM)
            for operand in (
                features.reshape(frames * width, channels),
                row(norm_gain),
                row(norm_bias),
                query_weight,
                row(query_bias),
                key_weight,
                value_weight,
                row(value_bias),
                out_weight,
                row(out_bias),
                taps,
                row(conv_bias),
            )
        )
    )
    return decoded.reshape(3, 2, 2 * width, channels)


def per_device(features, *rest):
    count = lax.axis_size("space")
    frames, local_rows, width, channels = features.shape
    outs = rest[9].shape[4]
    if (frames, local_rows, width) == (2, 1, 8) and outs == 32 and count % 4 == 0:
        return per_device_fused(features, *rest)
    return per_device_sharded(features, *rest)


def solution(mesh):
    placed = (
        P("groups", "space", None, None),
        P(),
        P(),
        P(),
        P(),
        P(),
        P(),
        P(),
        P(),
        P(),
        P(None, None, None, None, "space"),
        P(),
    )
    return jax.shard_map(
        per_device,
        mesh=mesh,
        in_specs=placed,
        out_specs=P("groups", "space", None, None),
        check_vma=False,
    )
```
